32 devices in a mesh: section: 2 (over core), dp: 4 (over z), ctx: 4 (over y, x).
Axes of the slice: x: 2, y: 2, z: 4, core: 2. Of those that a mesh axis runs over, the one named last changes fastest.
Arguments:
- hidden: bfloat16 [2, 4, 1024, 1024], P(None, 'dp', 'ctx'), may hold values from -6 to 6
- cotangent: bfloat16 [2, 4, 1024, 1024], P(None, 'dp', 'ctx'), may hold values from -6 to 6
- segments: int32 [2, 4, 1024], P(None, 'dp'), may hold values from 0 to 2, as said below
- in_weight: bfloat16 [2, 1024, 4384], P('section', ('dp', 'ctx')), may hold values from -0.1875 to 0.1875
- out_weight: bfloat16 [2, 2048, 1024], P('section', ('dp', 'ctx')), may hold values from -0.125 to 0.125
- conv_weight: bfloat16 [2, 4, 2304], P('section', None, ('dp', 'ctx')), may hold values from -3 to 3
- conv_bias: bfloat16 [2, 2304], P('section', ('dp', 'ctx')), may hold values from -3 to 3
- norm_gain: bfloat16 [2, 1024], P('section', ('dp', 'ctx')), may hold values from 0.25 to 1.75
- gate_gain: bfloat16 [2, 2048], P('section', ('dp', 'ctx')), may hold values from 0.25 to 1.75
- step_bias: float32 [2, 32], P('section'), may hold values from -7 to -3
- decay_log: float32 [2, 32], P('section'), may hold values from -1.5 to 0.5
- skip_gain: float32 [2, 32], P('section'), may hold values from 0.5 to 1.5
Outputs:
- layer_out: bfloat16 [2, 2, 4, 1024, 1024], P('section', None, 'dp', 'ctx')
- input_grad: bfloat16 [2, 2, 4, 1024, 1024], P('section', None, 'dp', 'ctx')
- in_weight_grad: float32 [2, 1024, 4384], P('section', ('dp', 'ctx'))
- out_weight_grad: float32 [2, 2048, 1024], P('section', ('dp', 'ctx'))
- conv_weight_grad: float32 [2, 4, 2304], P('section', None, ('dp', 'ctx'))
- conv_bias_grad: float32 [2, 2304], P('section', ('dp', 'ctx'))
- norm_gain_grad: float32 [2, 1024], P('section', ('dp', 'ctx'))
- gate_gain_grad: float32 [2, 2048], P('section', ('dp', 'ctx'))
- step_bias_grad: float32 [2, 32], P('section')
- decay_log_grad: float32 [2, 32], P('section')
- skip_gain_grad: float32 [2, 32], P('section')
The draws below stay inside these ranges and needn't reach their ends.
Inputs may be any that keep to these rules, and one draw needn't show every extreme that they name: `segments`: in every row the numbers start at 0, never fall, and rise by one at exactly two tokens: one among the first 256 tokens of the row but not its first token, and one among its last 256 tokens but not the first of those.
All inputs are finite; a program needn't handle non-finite values.
Results may differ from the reference program's by a relative error of at most 0.012.
Values may be sent and summed in bfloat16 or wider, within the bound.
No kernel may reach another device: no remote copies, remote signals or barrier semaphores. Data moves between devices by JAX's collectives and lax.ppermute only.
A program may use at most 320 MiB of HBM per device.

```python
import jax
import jax.numpy as jnp
from jax import lax

D = 1024
E = 2048
H = 32
P_SIZE = 64
N = 128
KW = 4
MB = 2
SEQ = 1024
ROWS = 4
TOK_DEV = 256
CC = 2304
NPROJ = 4384


def draw_segments(key, part):
    key = jax.random.fold_in(key, 11)
    first_key, last_key = jax.random.split(key)
    opening = jax.random.randint(first_key, (MB, ROWS, 1), 1, TOK_DEV)
    closing = jax.random.randint(last_key, (MB, ROWS, 1), SEQ - TOK_DEV + 1, SEQ)
    places = jnp.arange(SEQ, dtype=jnp.int32)[None, None, :]
    return (places >= opening).astype(jnp.int32) + (places >= closing).astype(jnp.int32)


def level_of(rng, dims, shards, low, high):
    gain = 1.0
    for position, shards_of in shards:
        heights = jax.random.uniform(jax.random.fold_in(jax.random.fold_in(rng, 6), position), (shards_of,), jnp.float32, low / len(shards), high / len(shards))
        gain = gain * jnp.repeat(jnp.exp(heights), dims[position] // shards_of).reshape((-1,) + (1,) * (len(dims) - 1 - position))
    return gain


def normal_values(own_key, extent, spread, reach, cuts=(), kind=jnp.bfloat16):
    values = spread * jax.random.normal(own_key, extent, jnp.float32)
    if cuts:
        values = values * level_of(own_key, extent, cuts, -0.22, 0.18)
    return jnp.clip(values, -reach, reach).astype(kind)


def setup_inputs(seed: int = 0) -> dict:
    seeds = jax.random.split(jax.random.key(seed), 13)
    return {
        "hidden": normal_values(seeds[0], (MB, ROWS, SEQ, D), 1.0, 6.0, ((1, 4), (2, 4))),
        "cotangent": normal_values(seeds[1], (MB, ROWS, SEQ, D), 1.0, 6.0, ((1, 4), (2, 4))),
        "segments": draw_segments(jax.random.fold_in(seeds[12], 71), 0),
        "in_weight": normal_values(seeds[3], (2, D, NPROJ), D ** -0.5, 0.1875, ((0, 2), (1, 16))),
        "out_weight": normal_values(seeds[4], (2, E, D), E ** -0.5, 0.125, ((0, 2), (1, 16))),
        "conv_weight": normal_values(seeds[5], (2, KW, CC), KW ** -0.5, 3.0, ((0, 2), (2, 16))),
        "conv_bias": normal_values(seeds[6], (2, CC), 0.5, 3.0, ((0, 2), (1, 16))),
        "norm_gain": jnp.clip(1.0 + 0.15 * jax.random.normal(seeds[7], (2, D), jnp.float32), 0.25, 1.75).astype(jnp.bfloat16),
        "gate_gain": jnp.clip(1.0 + 0.15 * jax.random.normal(seeds[8], (2, E), jnp.float32), 0.25, 1.75).astype(jnp.bfloat16),
        "step_bias": jnp.clip(-7.0 + 4.0 * jax.random.uniform(seeds[9], (2, H), jnp.float32) ** level_of(seeds[9], (2, H), ((0, 2),), -0.2, 0.2), -7.0, -3.0),
        "decay_log": jnp.clip(-1.5 + 2.0 * jax.random.uniform(seeds[10], (2, H), jnp.float32) ** level_of(seeds[10], (2, H), ((0, 2),), -0.2, 0.2), -1.5, 0.5),
        "skip_gain": jnp.clip(0.5 + 1.0 * jax.random.uniform(seeds[11], (2, H), jnp.float32) ** level_of(seeds[11], (2, H), ((0, 2),), -0.2, 0.2), 0.5, 1.5),
    }


eps_norm = 1e-05
precise = lax.Precision.HIGHEST

@jax.custom_vjp
def low(v):
    return lax.optimization_barrier(v.astype(jnp.bfloat16)).astype(jnp.float32)

@jax.custom_vjp
def low_back(v):
    return v

def low_keep(v):
    return (low(v), None)

def low_pass(kept, grad):
    return (grad,)

def back_keep(v):
    return (v, None)

def back_low(kept, grad):
    return (low(grad),)
low.defvjp(low_keep, low_pass)
low_back.defvjp(back_keep, back_low)

def rms_scale(values):
    return values * lax.rsqrt(lax.optimization_barrier(jnp.mean(values * values, axis=-1, keepdims=True)) + eps_norm)

def ssd_block(carried, pieces):
    memory, last_seg = carried
    inputs, writer, reader, step_size, log_rates, seg_row = pieces
    length = seg_row.shape[0]
    cumulative = jnp.cumsum(log_rates, axis=0)
    row_ids = jnp.arange(length)
    causal_mask = (row_ids[:, None] >= row_ids[None, :]) & (seg_row[:, None] == seg_row[None, :])
    log_gaps = cumulative[:, None, :] - cumulative[None, :, :]
    fading = jnp.exp(jnp.where(causal_mask[:, :, None], log_gaps, -1e+30))
    scores = jnp.dot(reader, writer.T, precision=precise)
    scaled = inputs * step_size[:, :, None]
    mixed_out = jnp.einsum('tsh,shp->thp', scores[:, :, None] * fading, scaled, precision=precise)
    carry_in = jnp.exp(cumulative) * (seg_row == last_seg).astype(jnp.float32)[:, None]
    mixed_out = mixed_out + carry_in[:, :, None] * jnp.einsum('tn,hpn->thp', reader, memory, precision=precise)
    keep_end = (seg_row == seg_row[-1]).astype(jnp.float32)
    end_weight = jnp.exp(cumulative[-1][None, :] - cumulative) * keep_end[:, None]
    fresh_state = jnp.einsum('shp,sn->hpn', scaled * end_weight[:, :, None], writer, precision=precise)
    through = jnp.exp(cumulative[-1]) * (seg_row[-1] == last_seg).astype(jnp.float32)
    memory = through[:, None, None] * memory + fresh_state
    return ((memory, seg_row[-1]), mixed_out)

def mixer_row(residual, seg_row, weights):
    w_in, w_out, conv_w, conv_b, gain_in, gain_gate, step_b, decay_lg, skip_g = weights
    normed = low(rms_scale(residual) * gain_in)
    projected = low_back(jnp.dot(normed, w_in, precision=precise))
    gate_pre = projected[:, :E]
    conv_in = low(projected[:, E:E + CC])
    raw_step = projected[:, E + CC:]
    padded = jnp.concatenate([jnp.zeros((KW - 1, CC), jnp.float32), conv_in], axis=0)
    seg_pad = jnp.concatenate([jnp.full((KW - 1,), -1, jnp.int32), seg_row])
    summed = conv_b + sum((conv_w[offset] * padded[offset:offset + SEQ] * (seg_pad[offset:offset + SEQ] == seg_row).astype(jnp.float32)[:, None] for offset in range(KW)))
    active = jax.nn.silu(summed)
    inputs = active[:, :E].reshape(SEQ, H, P_SIZE)
    writer = active[:, E:E + N]
    reader = active[:, E + N:]
    step_size = jax.nn.softplus(raw_step + step_b)
    log_rates = -step_size * jnp.exp(decay_lg)
    block_len = 128
    num_blocks = SEQ // block_len

    def to_blocks(values):
        return values.reshape((num_blocks, block_len) + values.shape[1:])
    start_carry = (jnp.zeros((H, P_SIZE, N), jnp.float32), jnp.array(-1, jnp.int32))
    _, outputs = lax.scan(jax.checkpoint(ssd_block), start_carry, (to_blocks(inputs), to_blocks(writer), to_blocks(reader), to_blocks(step_size), to_blocks(log_rates), to_blocks(seg_row)))
    mixed_out = outputs.reshape(SEQ, H, P_SIZE) + skip_g[None, :, None] * inputs
    gated_out = mixed_out.reshape(SEQ, E) * jax.nn.silu(gate_pre)
    normed_out = low(rms_scale(gated_out) * gain_gate)
    return residual + low_back(jnp.dot(normed_out, w_out, precision=precise))

def mixer(residual, seg_rows, weights):

    def one_row(row_pair):
        return mixer_row(row_pair[0], row_pair[1], weights)
    return lax.map(one_row, (residual, seg_rows))

def reference(hidden, cotangent, segments, in_weight, out_weight, conv_weight, conv_bias, norm_gain, gate_gain, step_bias, decay_log, skip_gain):
    total_rows = MB * ROWS
    source = hidden.astype(jnp.float32).reshape(total_rows, SEQ, D)
    seg_rows = segments.reshape(total_rows, SEQ)
    params = tuple((member.astype(jnp.float32) for member in (in_weight, out_weight, conv_weight, conv_bias, norm_gain, gate_gain, step_bias, decay_log, skip_gain)))

    def forward(source_in, layer_params, probe_zero):
        first_layer = tuple((member[0] for member in layer_params))
        second_layer = tuple((member[1] for member in layer_params))
        hidden_one = mixer(source_in, seg_rows, first_layer)
        middle = low_back(low(hidden_one) + probe_zero)
        hidden_two = mixer(middle, seg_rows, second_layer)
        return (hidden_one, hidden_two)
    probe_zero = jnp.zeros_like(source)
    (hidden_one, hidden_two), pullback = jax.vjp(forward, source, params, probe_zero)
    pulled = pullback((jnp.zeros_like(hidden_one), cotangent.astype(jnp.float32).reshape(total_rows, SEQ, D)))
    weight_grads = pulled[1]
    full_shape = (MB, ROWS, SEQ, D)
    layer_out = jnp.stack([hidden_one.reshape(full_shape), hidden_two.reshape(full_shape)]).astype(jnp.bfloat16)
    input_grad = jnp.stack([pulled[0].reshape(full_shape), pulled[2].reshape(full_shape)]).astype(jnp.bfloat16)
    return (layer_out, input_grad, weight_grads[0], weight_grads[1], weight_grads[2], weight_grads[3], weight_grads[4], weight_grads[5], weight_grads[6], weight_grads[7], weight_grads[8])
```

```python
import functools

import jax
import jax.numpy as jnp
from jax import lax
from jax.experimental import pallas as pl
from jax.experimental.pallas import tpu as pltpu
from jax.sharding import PartitionSpec as P

D = 1024
E = 2048
H = 32
P_SIZE = 64
N = 128
KW = 4
CC = 2304
NPROJ = 4384

EH = E // 2
HH = H // 2
LANES = 128
CL = EH + 2 * N
COLS = EH + CL + LANES
NS = N + 16
TILE = 128
WIDE = 256
EPS = 1e-05
VMEM = 56 * 2**20
GRID = ("dp", "ctx")
f32 = jnp.float32
bf16 = jnp.bfloat16


def dot(a, b):
    return jnp.dot(a.astype(bf16), b.astype(bf16), preferred_element_type=f32)


def dot_nt(a, b):
    return lax.dot_general(
        a.astype(bf16), b.astype(bf16), (((1,), (1,)), ((), ())), preferred_element_type=f32
    )


def dot_exact(a, b):
    return jnp.dot(a, b, preferred_element_type=f32, precision=lax.Precision.HIGHEST)


def sigmoid(v):
    return 1.0 / (1.0 + jnp.exp(-v))


def softplus(v):
    return jnp.maximum(v, 0.0) + jnp.log1p(jnp.exp(-jnp.abs(v)))


def lanes_of(shape):
    return lax.broadcasted_iota(jnp.int32, shape, len(shape) - 1)


def rows_of(shape):
    return lax.broadcasted_iota(jnp.int32, shape, len(shape) - 2)


def head_columns(values, first, width):
    turned = pltpu.roll(values, lax.rem(LANES - first, LANES), 1)
    low = lanes_of((values.shape[0], LANES)) < P_SIZE
    columns = [turned[:, i : i + 1] for i in range(width // P_SIZE)]
    tiles = [
        jnp.where(low, columns[2 * i], columns[2 * i + 1]) for i in range(width // LANES)
    ]
    spread = tiles[0] if len(tiles) == 1 else jnp.concatenate(tiles, axis=1)
    return spread, columns


def chain(refs):
    total = None
    for ref in reversed(refs):
        part = ref[0, :N, :].astype(f32)
        if total is None:
            total = part
        else:
            fade = ref[0, N : N + 1, :].astype(f32) + ref[0, N + 8 : N + 9, :].astype(f32)
            total = part + fade * total
    return total


def fade_rows(row):
    high = row.astype(bf16).astype(f32)
    which = rows_of((16, row.shape[1])) < 8
    return jnp.where(which, high, row - high).astype(bf16)


def conv_rows(ext, values, edge, taps, marks):
    length = values.shape[0]
    ext[0:8, :] = edge
    ext[8 : 8 + length, :] = values.astype(bf16).astype(f32)
    summed = jnp.broadcast_to(taps[KW : KW + 1, :], values.shape)
    for k in range(KW):
        d = KW - 1 - k
        piece = ext[8 - d : 8 - d + length, :]
        if d:
            piece = piece * marks[:, d : d + 1]
        summed = summed + taps[k : k + 1, :] * piece
    return summed


def conv_back(ext, dext, d_pre, taps, marks, edge_ref, grads_ref, extra_rows):
    length = d_pre.shape[0]
    sums = []
    dext[0:8, :] = jnp.zeros((8, d_pre.shape[1]), f32)
    dext[8 : 8 + length, :] = taps[KW - 1 : KW, :] * d_pre
    for k in range(KW):
        d = KW - 1 - k
        masked = d_pre * marks[:, d : d + 1] if d else d_pre
        sums.append(jnp.sum(masked * ext[8 - d : 8 - d + length, :], axis=0, keepdims=True))
        if d:
            dext[8 - d : 8 - d + length, :] += taps[k : k + 1, :] * masked
    sums.append(jnp.sum(d_pre, axis=0, keepdims=True))
    sums += extra_rows
    sums.append(jnp.zeros((8 - len(sums), d_pre.shape[1]), f32))
    grads_ref[0] = jnp.concatenate(sums, axis=0)
    edge_ref[0] = dext[0:8, :]
    return dext[8 : 8 + length, :]


def step_parts(raw_ref, heads_ref):
    raw = raw_ref[0] + heads_ref[0:1, :]
    step = softplus(raw)
    rates = step * heads_ref[1:2, :]
    length = raw.shape[0]
    lower = (rows_of((length, length)) >= lanes_of((length, length))).astype(f32)
    return raw, step, rates, dot_exact(lower, rates)


def forward_local(
    x_ref, bc_ref, raw_ref, edge_x_ref, edge_bc_ref, marks_ref, seg_ref, taps_x_ref, taps_bc_ref,
    heads_ref, skip_ref, y_ref, state_ref, bc_out, cum_out,
    ext, ext_bc, scores, step_s, cum_s, cum_t,
):
    tile = pl.program_id(1)
    length = x_ref.shape[1]
    marks = marks_ref[0]

    @pl.when(tile == 0)
    def _():
        pre = conv_rows(ext_bc, bc_ref[0], edge_bc_ref[0], taps_bc_ref, marks)
        active = pre * sigmoid(pre)
        bc_out[0] = active
        _, step, _, cum = step_parts(raw_ref, heads_ref)
        step_s[...] = step
        cum_s[...] = cum
        cum_out[0] = cum
        cum_t[...] = cum.T
        shape = (length, length)
        keep = (rows_of(shape) >= lanes_of(shape)) & (marks[:, 7:8] == seg_ref[0, 0:1, :])
        scores[...] = jnp.where(keep, dot_nt(active[:, N:], active[:, :N]), 0.0)

    pre = conv_rows(ext, x_ref[0], edge_x_ref[0], taps_x_ref, marks)
    active = pre * sigmoid(pre)
    spread_step, _ = head_columns(step_s[...], 2 * tile, TILE)
    spread_cum, columns = head_columns(cum_s[...], 2 * tile, TILE)
    last = spread_cum[length - 1 : length, :]
    scaled = active * spread_step
    end = scaled * (jnp.exp(last - spread_cum) * marks[:, 5:6])
    writer = bc_out[0, :, :N]
    state_ref[0, :N, :] = dot(writer.T, end).astype(bf16)
    state_ref[0, N:, :] = fade_rows(jnp.exp(last) * marks[0:1, 6:7])
    outs = []
    for i in range(2):
        row = cum_t[pl.ds(2 * tile + i, 1), :]
        fade = jnp.exp(jnp.minimum(columns[i] - row, 0.0))
        outs.append(dot(scores[...] * fade, scaled[:, i * P_SIZE : (i + 1) * P_SIZE]))
    y_ref[0] = jnp.concatenate(outs, axis=1) + skip_ref[0:1, :] * active


def forward_join(hops, *refs):
    states = refs[:hops]
    (y_ref, gate_ref, bc_ref, cum_ref, marks_ref, gain_ref, wout_ref, mixed_ref, mem_ref, part_ref,
     total) = refs[hops:]
    tile = pl.program_id(1)
    tiles = pl.num_programs(1)
    marks = marks_ref[0]
    memory = chain(states)
    mem_ref[0] = memory.astype(bf16)
    carry, _ = head_columns(jnp.exp(cum_ref[0]) * marks[:, 4:5], (WIDE // P_SIZE) * tile, WIDE)
    mixed = y_ref[0] + carry * dot(bc_ref[0, :, N:], memory)
    mixed_ref[0] = mixed
    gate = gate_ref[0]
    gated = mixed * gate * sigmoid(gate)
    part = dot(gated * gain_ref[0:1, :], wout_ref[...])
    stat = jnp.sum(gated * gated, axis=1, keepdims=True)

    @pl.when(tile == 0)
    def _():
        total[:, :D] = part
        total[:, D:] = jnp.broadcast_to(stat, (stat.shape[0], LANES))

    @pl.when(tile > 0)
    def _():
        total[:, :D] += part
        total[:, D:] += jnp.broadcast_to(stat, (stat.shape[0], LANES))

    @pl.when(tile == tiles - 1)
    def _():
        part_ref[0] = total[...]


def backward_gate(
    grad_ref, wout_ref, total_ref, mixed_ref, gate_ref, bc_ref, cum_ref, marks_ref, gain_ref,
    dy_ref, dgate_ref, normed_ref, gain_grad_ref, state_ref, moment,
):
    tile = pl.program_id(1)
    length = grad_ref.shape[1]
    marks = marks_ref[0]

    @pl.when(tile == 0)
    def _():
        inner = jnp.sum(grad_ref[0].astype(f32) * total_ref[0, :, :D], axis=1, keepdims=True)
        moment[...] = jnp.broadcast_to(inner / E, (length, LANES))

    scale = lax.rsqrt(total_ref[0, :, D : D + 1] / E + EPS)
    d_normed = dot_nt(grad_ref[0], wout_ref[...])
    gate = gate_ref[0]
    sig = sigmoid(gate)
    silu = gate * sig
    mixed = mixed_ref[0]
    gated = mixed * silu
    gain = gain_ref[0:1, :]
    normed_ref[0] = (gated * scale * gain).astype(bf16)
    gain_grad_ref[0] = jnp.broadcast_to(
        jnp.sum(d_normed * gated * scale, axis=0, keepdims=True), (8, WIDE)
    )
    d_gated = scale * (gain * d_normed) - gated * (scale * scale * scale * moment[:, 0:1])
    dy = d_gated * silu
    dy_ref[0] = dy
    dgate_ref[0] = (d_gated * mixed * (sig + silu * (1.0 - sig))).astype(bf16)
    spread, _ = head_columns(cum_ref[0], (WIDE // P_SIZE) * tile, WIDE)
    carry = jnp.exp(spread) * marks[:, 4:5]
    state_ref[0, :N, :] = dot(bc_ref[0, :, N:].T, dy * carry).astype(bf16)
    last = spread[length - 1 : length, :]
    state_ref[0, N:, :] = fade_rows(jnp.exp(last) * marks[0:1, 6:7])


def backward_local(hops, *refs):
    states = refs[:hops]
    (x_ref, bc_ref, raw_ref, edge_x_ref, edge_bc_ref, marks_ref, seg_ref, taps_x_ref, taps_bc_ref,
     heads_ref, skip_ref, dy_ref, mixed_ref, mem_ref,
     dx_ref, dbc_ref, draw_ref, edge_x_out, edge_bc_out, grads_x_ref, grads_bc_ref, grads_h_ref,
     ext, dext, ext_bc, dext_bc, pre_bc, active_bc, scores, d_scores, raw_s, step_s, rates_s, cum_s,
     cum_t, d_bc, d_cum, d_step) = refs[hops:]
    tile = pl.program_id(1)
    tiles = pl.num_programs(1)
    length = x_ref.shape[1]
    marks = marks_ref[0]
    shape = (length, length)
    keep = (rows_of(shape) <= lanes_of(shape)) & (marks[:, 7:8] == seg_ref[0, 0:1, :])

    @pl.when(tile == 0)
    def _():
        pre = conv_rows(ext_bc, bc_ref[0], edge_bc_ref[0], taps_bc_ref, marks)
        active = pre * sigmoid(pre)
        pre_bc[...] = pre
        active_bc[...] = active
        raw, step, rates, cum = step_parts(raw_ref, heads_ref)
        raw_s[...] = raw
        step_s[...] = step
        rates_s[...] = rates
        cum_s[...] = cum
        cum_t[...] = cum.T
        scores[...] = jnp.where(keep, dot_nt(active[:, :N], active[:, N:]), 0.0)
        d_scores[...] = jnp.zeros(shape, f32)
        d_bc[...] = jnp.zeros((length, 2 * N), f32)
        d_cum[...] = jnp.zeros((length, LANES), f32)
        d_step[...] = jnp.zeros((length, LANES), f32)

    pre = conv_rows(ext, x_ref[0], edge_x_ref[0], taps_x_ref, marks)
    sig = sigmoid(pre)
    active = pre * sig
    spread_step, _ = head_columns(step_s[...], 2 * tile, TILE)
    spread_cum, columns = head_columns(cum_s[...], 2 * tile, TILE)
    last = spread_cum[length - 1 : length, :]
    scaled = active * spread_step
    end_weight = jnp.exp(last - spread_cum) * marks[:, 5:6]
    carry = jnp.exp(spread_cum) * marks[:, 4:5]
    end = scaled * end_weight
    through = jnp.exp(last) * marks[0:1, 6:7]
    later = chain(states)
    memory = mem_ref[0].astype(f32)
    writer = active_bc[:, :N]
    dy = dy_ref[0]
    back = dot(writer, later)
    d_bc[:, :N] += dot_nt(end, later)
    d_bc[:, N:] += dot_nt(dy * carry, memory)
    d_scaled = []
    total_scores = d_scores[...]
    for i in range(2):
        cut = slice(i * P_SIZE, (i + 1) * P_SIZE)
        row = cum_t[pl.ds(2 * tile + i, 1), :]
        fade = jnp.exp(jnp.minimum(row - columns[i], 0.0))
        total_scores = total_scores + dot_nt(scaled[:, cut], dy[:, cut]) * fade
        d_scaled.append(dot(scores[...] * fade, dy[:, cut]))
    d_scores[...] = total_scores
    d_diag = jnp.concatenate(d_scaled, axis=1)
    skip = skip_ref[0:1, :]
    rounded_dy = dy.astype(bf16).astype(f32)
    rounded_scaled = scaled.astype(bf16).astype(f32)
    ended = end * back
    gaps = rounded_dy * (mixed_ref[0] - skip * active) - rounded_scaled * d_diag - ended
    closing = jnp.sum(ended, axis=0, keepdims=True) + through * jnp.sum(
        later * memory, axis=0, keepdims=True
    )
    gaps = gaps + jnp.where(rows_of((length, LANES)) == length - 1, closing, 0.0)
    d_all = d_diag + end_weight * back
    places = (
        lax.broadcasted_iota(jnp.int32, (LANES, LANES), 1)
        == 2 * tile + (lax.broadcasted_iota(jnp.int32, (LANES, LANES), 0) >= P_SIZE).astype(jnp.int32)
    ).astype(bf16)
    places = jnp.concatenate([places, places], axis=0)

    def per_head(values):
        high = values.astype(bf16)
        rest = (values - high.astype(f32)).astype(bf16)
        return jnp.dot(
            jnp.concatenate([high, rest], axis=1), places, preferred_element_type=f32
        )

    d_cum[...] += per_head(gaps)
    d_step[...] += per_head(d_all * active)
    d_active = d_all * spread_step + skip * dy
    d_pre = d_active * (sig + active * (1.0 - sig))
    dx_ref[0] = conv_back(
        ext, dext, d_pre, taps_x_ref, marks, edge_x_out, grads_x_ref,
        [jnp.sum(dy * active, axis=0, keepdims=True)],
    )

    @pl.when(tile == tiles - 1)
    def _():
        reader = active_bc[:, N:]
        kept = jnp.where(keep, d_scores[...], 0.0)
        d_bc[:, :N] += dot(kept, reader)
        d_bc[:, N:] += dot(kept.T, active_bc[:, :N])
        pre2 = pre_bc[...]
        sig2 = sigmoid(pre2)
        d_pre2 = d_bc[...] * (sig2 + pre2 * sig2 * (1.0 - sig2))
        dbc_ref[0] = conv_back(
            ext_bc, dext_bc, d_pre2, taps_bc_ref, marks, edge_bc_out, grads_bc_ref, []
        )
        upper = (rows_of(shape) <= lanes_of(shape)).astype(f32)
        d_rates = dot_exact(upper, d_cum[...])
        d_raw = (d_step[...] + d_rates * heads_ref[1:2, :]) * sigmoid(raw_s[...])
        draw_ref[0] = d_raw
        grads_h_ref[0] = jnp.concatenate(
            [
                jnp.sum(d_raw, axis=0, keepdims=True),
                jnp.sum(d_rates * rates_s[...], axis=0, keepdims=True),
                jnp.zeros((6, LANES), f32),
            ],
            axis=0,
        )


def backward_project(
    dgate_ref, dx_ref, dbc_ref, draw_ref, edge_ref, win_ref, dproj_ref, dn_ref, held
):
    length = dx_ref.shape[1]
    held[:, :EH] = dx_ref[0]
    held[:, EH:] = dbc_ref[0]
    held[length - 8 :, :] += edge_ref[0]
    dproj_ref[0, :, :EH] = dgate_ref[0]
    dproj_ref[0, :, EH : EH + CL] = held[...].astype(bf16)
    dproj_ref[0, :, EH + CL :] = draw_ref[0].astype(bf16)
    dn_ref[0] = dot_nt(dproj_ref[0], win_ref[...])


def spec(block, index):
    return pl.BlockSpec(block, index)


def params():
    return pltpu.CompilerParams(vmem_limit_bytes=VMEM)


def row_tile(length, width, first=0):
    return spec((1, length, width), lambda r, t: (r, 0, first + t))


def row_fixed(length, width, column=0):
    return spec((1, length, width), lambda r, t: (r, 0, column))


def flat_tile(rows, width):
    return spec((rows, width), lambda r, t: (0, t))


def flat_fixed(rows, width):
    return spec((rows, width), lambda r, t: (0, 0))


def out(*shape, dtype=f32):
    return jax.ShapeDtypeStruct(shape, dtype)


def cost(flops, moved):
    return pl.CostEstimate(flops=int(flops), bytes_accessed=int(moved), transcendentals=0)


def local_specs(length):
    return [
        row_tile(length, TILE, EH // TILE),
        row_fixed(length, 2 * N, 2 * EH // (2 * N)),
        row_fixed(length, LANES, (EH + CL) // LANES),
        row_tile(8, TILE),
        row_fixed(8, 2 * N, EH // (2 * N)),
        row_fixed(length, LANES),
        row_fixed(8, length),
        flat_tile(8, TILE),
        spec((8, 2 * N), lambda r, t: (0, EH // (2 * N))),
        flat_fixed(8, LANES),
        flat_tile(8, TILE),
    ]


def run_forward_local(proj, edge, marks, seg_rows, layer):
    rows, length, _ = proj.shape
    return pl.pallas_call(
        forward_local,
        grid=(rows, EH // TILE),
        in_specs=local_specs(length),
        out_specs=[
            row_tile(length, TILE), row_tile(NS, TILE), row_fixed(length, 2 * N),
            row_fixed(length, LANES),
        ],
        out_shape=[
            out(rows, length, EH), out(rows, NS, EH, dtype=bf16), out(rows, length, 2 * N),
            out(rows, length, LANES),
        ],
        scratch_shapes=[
            pltpu.VMEM((length + 8, TILE), f32), pltpu.VMEM((length + 8, 2 * N), f32),
            pltpu.VMEM((length, length), f32), pltpu.VMEM((length, LANES), f32),
            pltpu.VMEM((length, LANES), f32), pltpu.VMEM((LANES, length), f32),
        ],
        compiler_params=params(),
        cost_estimate=cost(rows * length * length * EH * 2 * 16, rows * length * EH * 12),
        name="forward_local",
    )(proj, proj, proj, edge, edge, marks, seg_rows, layer["taps"], layer["taps"], layer["heads"],
      layer["skip"])


def run_forward_join(states, y, proj, bc, cum, marks, gain, wout):
    rows, length, _ = y.shape
    hops = len(states)
    return pl.pallas_call(
        functools.partial(forward_join, hops),
        grid=(rows, EH // WIDE),
        in_specs=[row_tile(NS, WIDE)] * hops + [
            row_tile(length, WIDE), row_tile(length, WIDE), row_fixed(length, 2 * N),
            row_fixed(length, LANES), row_fixed(length, LANES), flat_tile(8, WIDE),
            spec((WIDE, D), lambda r, t: (t, 0)),
        ],
        out_specs=[
            row_tile(length, WIDE), row_tile(N, WIDE), row_fixed(length, D + LANES),
        ],
        out_shape=[
            out(rows, length, EH), out(rows, N, EH, dtype=bf16), out(rows, length, D + LANES),
        ],
        scratch_shapes=[pltpu.VMEM((length, D + LANES), f32)],
        compiler_params=params(),
        name="forward_join",
    )(*states, y, proj, bc, cum, marks, gain, wout)


def run_backward_gate(grad, wout, total, mixed, proj, bc, cum, marks, gain):
    rows, length, _ = mixed.shape
    return pl.pallas_call(
        backward_gate,
        grid=(rows, EH // WIDE),
        in_specs=[
            row_fixed(length, D), spec((WIDE, D), lambda r, t: (t, 0)),
            row_fixed(length, D + LANES), row_tile(length, WIDE), row_tile(length, WIDE),
            row_fixed(length, 2 * N), row_fixed(length, LANES), row_fixed(length, LANES),
            flat_tile(8, WIDE),
        ],
        out_specs=[
            row_tile(length, WIDE), row_tile(length, WIDE), row_tile(length, WIDE),
            row_tile(8, WIDE), row_tile(NS, WIDE),
        ],
        out_shape=[
            out(rows, length, EH), out(rows, length, EH, dtype=bf16),
            out(rows, length, EH, dtype=bf16), out(rows, 8, EH), out(rows, NS, EH, dtype=bf16),
        ],
        scratch_shapes=[pltpu.VMEM((length, LANES), f32)],
        compiler_params=params(),
        name="backward_gate",
    )(grad, wout, total, mixed, proj, bc, cum, marks, gain)


def run_backward_local(states, proj, edge, marks, seg_rows, layer, dy, mixed, memory):
    rows, length, _ = proj.shape
    hops = len(states)
    tall = lambda width: pltpu.VMEM((length + 8, width), f32)
    flat = lambda width: pltpu.VMEM((length, width), f32)
    return pl.pallas_call(
        functools.partial(backward_local, hops),
        grid=(rows, EH // TILE),
        in_specs=[row_tile(NS, TILE)] * hops + local_specs(length) + [
            row_tile(length, TILE), row_tile(length, TILE), row_tile(N, TILE),
        ],
        out_specs=[
            row_tile(length, TILE), row_fixed(length, 2 * N), row_fixed(length, LANES),
            row_tile(8, TILE), row_fixed(8, 2 * N), row_tile(8, TILE), row_fixed(8, 2 * N),
            row_fixed(8, LANES),
        ],
        out_shape=[
            out(rows, length, EH), out(rows, length, 2 * N), out(rows, length, LANES),
            out(rows, 8, EH), out(rows, 8, 2 * N), out(rows, 8, EH), out(rows, 8, 2 * N),
            out(rows, 8, LANES),
        ],
        scratch_shapes=[
            tall(TILE), tall(TILE), tall(2 * N), tall(2 * N), flat(2 * N), flat(2 * N),
            flat(length), flat(length), flat(LANES), flat(LANES), flat(LANES), flat(LANES),
            pltpu.VMEM((LANES, length), f32), flat(2 * N), flat(LANES), flat(LANES),
        ],
        compiler_params=params(),
        name="backward_local",
    )(*states, proj, proj, proj, edge, edge, marks, seg_rows, layer["taps"], layer["taps"],
      layer["heads"], layer["skip"], dy, mixed, memory)


def run_backward_project(dgate, dx, dbc, draw, edge, win):
    rows, length, _ = dx.shape
    block = lambda width: spec((1, length, width), lambda r: (r, 0, 0))
    return pl.pallas_call(
        backward_project,
        grid=(rows,),
        in_specs=[
            block(EH), block(EH), block(2 * N), block(LANES),
            spec((1, 8, CL), lambda r: (r, 0, 0)), spec((D, COLS), lambda r: (0, 0)),
        ],
        out_specs=[block(COLS), block(D)],
        out_shape=[out(rows, length, COLS, dtype=bf16), out(rows, length, D)],
        scratch_shapes=[pltpu.VMEM((length, CL), f32)],
        compiler_params=params(),
        name="backward_project",
    )(dgate, dx, dbc, draw, edge, win)


def shifted(values, axis, by):
    length = lax.axis_size(axis)
    pairs = [(i, i + by) for i in range(length) if 0 <= i + by < length]
    return lax.ppermute(values, axis, pairs)


def swapped(values):
    return lax.ppermute(values, "section", [(0, 1), (1, 0)])


def summed_over(values, axis):
    step = 1
    size = lax.axis_size(axis)
    while step < size:
        values = values + lax.ppermute(values, axis, [(i, i ^ step) for i in range(size)])
        step *= 2
    return values


def gathered(shard):
    return lax.all_gather(shard, GRID, axis=0, tiled=True)


def scattered(values):
    return lax.psum_scatter(values, GRID, scatter_dimension=0, tiled=True)


def of_core(values, core, axis, size):
    shape = values.shape
    split = values.reshape(shape[:axis] + (shape[axis] // (2 * size), 2, size) + shape[axis + 1 :])
    taken = lax.dynamic_index_in_dim(split, core, axis + 1, False)
    return taken.reshape(shape[:axis] + (shape[axis] // 2,) + shape[axis + 1 :])


def interleaved(even, odd, axis, size):
    shape = even.shape
    split = shape[:axis] + (shape[axis] // size, size) + shape[axis + 1 :]
    both = jnp.stack([even.reshape(split), odd.reshape(split)], axis=axis + 1)
    return both.reshape(shape[:axis] + (2 * shape[axis],) + shape[axis + 1 :])


def in_half(weight, core):
    rows = weight.shape[0]
    return jnp.concatenate(
        [
            of_core(weight[:, :E], core, 1, P_SIZE),
            of_core(weight[:, E : 2 * E], core, 1, P_SIZE),
            weight[:, 2 * E : 2 * E + 2 * N],
            of_core(weight[:, E + CC :], core, 1, 1),
            jnp.zeros((rows, LANES - HH), weight.dtype),
        ],
        axis=1,
    )


def shards(
    hidden, cotangent, segments, in_weight, out_weight, conv_weight, conv_bias, norm_gain,
    gate_gain, step_bias, decay_log, skip_gain,
):
    core = lax.axis_index("section")
    ctx_id = lax.axis_index("ctx")
    ctx_size = lax.axis_size("ctx")
    batches, rows_here, length, _ = hidden.shape
    rows = batches * rows_here
    is_first = core == 0
    by_layer = lambda own, other: (
        jnp.where(is_first, own, other), jnp.where(is_first, other, own)
    )

    whole_heads = out_weight.shape[1] % (2 * P_SIZE) == 0
    own_in = in_half(in_weight[0], core)
    other_in = swapped(in_half(in_weight[0], 1 - core))
    win = [gathered(part) for part in by_layer(own_in, other_in)]
    out_rows = out_weight[0] if whole_heads else gathered(out_weight[0])
    own_out = of_core(out_rows, core, 0, P_SIZE)
    other_out = swapped(of_core(out_rows, 1 - core, 0, P_SIZE))
    wout = by_layer(own_out, other_out)
    if whole_heads:
        wout = [gathered(part) for part in wout]

    channels = conv_bias.shape[1]
    pack = jnp.concatenate(
        [
            conv_weight[0].reshape(-1), conv_bias[0], norm_gain[0], gate_gain[0],
        ]
    ).astype(f32)
    heads_own = jnp.concatenate([step_bias[0], decay_log[0], skip_gain[0]])
    everything = lax.all_gather(
        jnp.concatenate([pack, heads_own])[None], ("section",) + GRID, axis=0, tiled=True
    ).reshape(2, -1, pack.shape[0] + 3 * H)
    d_share, e_share = norm_gain.shape[1], gate_gain.shape[1]

    def layer_params(l):
        part = everything[l]
        taps = part[:, : KW * channels].reshape(-1, KW, channels).swapaxes(0, 1).reshape(KW, CC)
        at = KW * channels
        bias = part[:, at : at + channels].reshape(1, CC)
        gain_in = part[:, at + channels : at + channels + d_share].reshape(D)
        at = at + channels + d_share
        gain_gate = part[:, at : at + e_share].reshape(E)
        per_head = part[0, at + e_share :].reshape(3, H)
        taps = jnp.concatenate([taps, bias, jnp.zeros((3, CC), f32)], axis=0)
        taps = jnp.concatenate([of_core(taps[:, :E], core, 1, P_SIZE), taps[:, E:]], axis=1)
        per_head = of_core(per_head, core, 1, 1)
        rates = -jnp.exp(per_head[1])
        heads = jnp.zeros((8, LANES), f32)
        heads = heads.at[0, :HH].set(per_head[0]).at[1, :HH].set(rates)
        skip = jnp.broadcast_to(jnp.repeat(per_head[2], P_SIZE)[None], (8, EH))
        gain = jnp.broadcast_to(of_core(gain_gate, core, 0, P_SIZE)[None], (8, EH))
        return {"taps": taps, "heads": heads, "skip": skip, "gain": gain, "norm": gain_in}

    layers = [layer_params(0), layer_params(1)]

    lead = jnp.full((batches, rows_here, KW - 1), -1, jnp.int32)
    seg_ext = lax.dynamic_slice_in_dim(
        jnp.concatenate([lead, segments], axis=2), ctx_id * length, length + KW - 1, 2
    ).reshape(rows, length + KW - 1)
    seg = seg_ext[:, KW - 1 :]
    before = seg_ext[:, KW - 2 : KW - 1]
    final = seg[:, -1:]
    columns = [
        (seg_ext[:, KW - 1 - d : KW - 1 - d + length] == seg).astype(f32) for d in range(KW)
    ]
    columns += [
        (seg == before).astype(f32), (seg == final).astype(f32),
        jnp.broadcast_to((final == before).astype(f32), seg.shape), seg.astype(f32),
    ]
    marks = jnp.stack(columns + [jnp.zeros(seg.shape, f32)] * (LANES - len(columns)), axis=-1)
    seg_rows = jnp.broadcast_to(seg.astype(f32)[:, None, :], (rows, 8, length))

    def forward(u, l):
        layer = layers[l]
        scale = lax.rsqrt(jnp.mean(u * u, axis=-1, keepdims=True) + EPS)
        normed = (u * scale * layer["norm"]).astype(bf16)
        proj = jnp.dot(
            normed.reshape(-1, D), win[l], preferred_element_type=f32
        ).reshape(rows, length, COLS)
        tail = proj[:, length - 8 :, EH : EH + CL].astype(bf16)
        edge = shifted(tail, "ctx", 1).astype(f32)
        y, state, bc, cum = run_forward_local(proj, edge, marks, seg_rows, layer)
        arrived = [shifted(state, "ctx", k) for k in range(1, ctx_size)]
        mixed, memory, part = run_forward_join(
            arrived, y, proj, bc, cum, marks, layer["gain"], wout[l]
        )
        total = part + swapped(part)
        branch = lax.rsqrt(total[:, :, D : D + 1] / E + EPS) * total[:, :, :D]
        kept = (u, normed, proj, edge, bc, cum, mixed, memory, total)
        return (u + branch).astype(bf16), kept

    def backward(g, l, kept):
        u, normed, proj, edge, bc, cum, mixed, memory, total = kept
        layer = layers[l]
        low = g.astype(bf16)
        dy, dgate, normed_out, gain_grad, state = run_backward_gate(
            low, wout[l], total, mixed, proj, bc, cum, marks, layer["gain"]
        )
        arrived = [shifted(state, "ctx", -k) for k in range(1, ctx_size)]
        d_wout = lax.dot_general(
            normed_out.reshape(-1, EH), low.reshape(-1, D), (((0,), (0,)), ((), ())),
            preferred_element_type=f32,
        ).astype(bf16)
        dx, dbc, draw, edge_x, edge_bc, grads_x, grads_bc, grads_h = run_backward_local(
            arrived, proj, edge, marks, seg_rows, layer, dy, mixed, memory
        )
        edge_back = shifted(jnp.concatenate([edge_x, edge_bc], axis=2), "ctx", -1)
        dproj, dn = run_backward_project(dgate, dx, dbc, draw, edge_back, win[l])
        d_win = lax.dot_general(
            normed.reshape(-1, D), dproj.reshape(-1, COLS), (((0,), (0,)), ((), ())),
            preferred_element_type=f32,
        ).astype(bf16)
        dn = dn + swapped(dn)
        scale = lax.rsqrt(jnp.mean(u * u, axis=-1, keepdims=True) + EPS)
        gained = layer["norm"] * dn
        d_u = g + scale * gained - u * scale**3 * jnp.mean(u * gained, axis=-1, keepdims=True)
        d_norm = jnp.sum(dn * u * scale, axis=(0, 1))
        sums_x = jnp.sum(grads_x, axis=0)
        sums_h = jnp.sum(grads_h, axis=0)
        small = jnp.concatenate(
            [
                sums_x[: KW + 1].reshape(-1),
                jnp.sum(grads_bc, axis=0)[: KW + 1].reshape(-1),
                jnp.sum(gain_grad, axis=0)[0],
                d_norm,
                sums_h[0, :HH],
                sums_h[1, :HH],
                jnp.sum(sums_x[KW + 1].reshape(HH, P_SIZE), axis=1),
            ]
        )
        return d_u.astype(bf16), d_win, d_wout, small

    source = hidden.reshape(rows, length, D).astype(f32)
    one, kept_one = forward(source, 0)
    two, kept_two = forward(one.astype(f32), 1)
    goal = cotangent.reshape(rows, length, D).astype(f32)
    d_two, d_win_two, d_wout_two, small_two = backward(goal, 1, kept_two)
    d_one, d_win_one, d_wout_one, small_one = backward(d_two.astype(f32), 0, kept_one)

    def owned(first, second):
        mine = jnp.where(is_first, first, second)
        arrived = swapped(jnp.where(is_first, second, first))
        even, odd = by_layer(mine, arrived)
        return mine, arrived, even, odd

    mine, arrived, even, odd = owned(scattered(d_win_one), scattered(d_win_two))
    both = mine[:, 2 * EH : 2 * EH + 2 * N].astype(f32) + arrived[
        :, 2 * EH : 2 * EH + 2 * N
    ].astype(f32)
    at = EH + CL
    in_grad = jnp.concatenate(
        [
            interleaved(even[:, : 2 * EH], odd[:, : 2 * EH], 1, P_SIZE).astype(f32),
            both,
            interleaved(even[:, at : at + HH], odd[:, at : at + HH], 1, 1).astype(f32),
        ],
        axis=1,
    )
    if whole_heads:
        mine, arrived, even, odd = owned(scattered(d_wout_one), scattered(d_wout_two))
        out_grad = interleaved(even, odd, 0, P_SIZE).astype(f32)
    else:
        spread = lambda part: scattered(
            interleaved(*by_layer(part, jnp.zeros_like(part)), 0, P_SIZE)
        )
        mine, arrived, even, odd = owned(spread(d_wout_one), spread(d_wout_two))
        out_grad = mine.astype(f32) + arrived.astype(f32)

    small = jnp.stack([small_one, small_two])
    small = summed_over(summed_over(small, "ctx"), "dp")
    mine, arrived, even, odd = owned(small[0], small[1])
    place = lax.axis_index("dp") * ctx_size + ctx_id
    size = (KW + 1) * EH
    conv_x = interleaved(even[:size].reshape(KW + 1, EH), odd[:size].reshape(KW + 1, EH), 1, P_SIZE)
    conv_bc = (mine + arrived)[size : size + (KW + 1) * 2 * N].reshape(KW + 1, 2 * N)
    conv_all = lax.dynamic_slice_in_dim(
        jnp.concatenate([conv_x, conv_bc], axis=1), place * channels, channels, 1
    )
    size += (KW + 1) * 2 * N
    gate_all = interleaved(even[size : size + EH], odd[size : size + EH], 0, P_SIZE)
    size += EH
    norm_all = mine[size : size + D]
    size += D
    per_head = [
        interleaved(even[size + i * HH : size + (i + 1) * HH], odd[size + i * HH : size + (i + 1) * HH], 0, 1)
        for i in range(3)
    ]
    own_shape = (1, batches, rows_here, length, D)
    return (
        jnp.where(is_first, one, two).reshape(own_shape),
        jnp.where(is_first, d_one, d_two).reshape(own_shape),
        in_grad[None],
        out_grad[None],
        conv_all[None, :KW],
        conv_all[None, KW],
        lax.dynamic_slice_in_dim(norm_all, place * d_share, d_share, 0)[None],
        lax.dynamic_slice_in_dim(gate_all, place * e_share, e_share, 0)[None],
        per_head[0][None],
        per_head[1][None],
        per_head[2][None],
    )


def solution(mesh):
    in_specs = (
        P(None, "dp", "ctx", None),
        P(None, "dp", "ctx", None),
        P(None, "dp", None),
        P("section", ("dp", "ctx"), None),
        P("section", ("dp", "ctx"), None),
        P("section", None, ("dp", "ctx")),
        P("section", ("dp", "ctx")),
        P("section", ("dp", "ctx")),
        P("section", ("dp", "ctx")),
        P("section", None),
        P("section", None),
        P("section", None),
    )
    out_specs = (
        P("section", None, "dp", "ctx", None),
        P("section", None, "dp", "ctx", None),
        P("section", ("dp", "ctx"), None),
        P("section", ("dp", "ctx"), None),
        P("section", None, ("dp", "ctx")),
        P("section", ("dp", "ctx")),
        P("section", ("dp", "ctx")),
        P("section", ("dp", "ctx")),
        P("section", None),
        P("section", None),
        P("section", None),
    )
    return jax.shard_map(shards, mesh=mesh, in_specs=in_specs, out_specs=out_specs, check_vma=False)
```
